512 devices in a mesh: fsdp: 32 (over y, z_hi), tp: 16 (over x, z_lo, core).
Axes of the slice: x: 4, y: 8, z: 8 (z_hi: 4, z_lo: 2; z = z_hi * 2 + z_lo), core: 2. Of those that a mesh axis runs over, the one named last changes fastest.
Arguments:
- acts: bfloat16 [8192, 4096], P('fsdp'), may hold values from -6 to 6
- cots: bfloat16 [8192, 14336], P('fsdp', 'tp'), may hold values from -6 to 6
- weight: bfloat16 [4096, 14336], P('fsdp', 'tp'), may hold values from -0.09375 to 0.09375
- basis_in: bfloat16 [32, 128, 128], P('fsdp'), may hold values from -0.5 to 0.5
- basis_out: bfloat16 [16, 896, 896], P('tp', 'fsdp'), may hold values from -0.1875 to 0.1875
- eigen_in: float32 [4096], P('fsdp'), may hold values from 0.2 to 5
- eigen_out: float32 [14336], P('tp'), may hold values from 0.2 to 5
- forget_rows: int32 [2048], P('fsdp'), may hold values from 0 to 255
- retain_rows: int32 [1024], P('fsdp'), may hold values from 0 to 255
Outputs:
- retained: bfloat16 [1024, 14336], P('fsdp', 'tp')
- back_grads: bfloat16 [1024, 4096], P('fsdp')
The draws below stay inside these ranges and needn't reach their ends.
All inputs are finite; a program needn't handle non-finite values.
Results may differ from the reference program's by a relative error of at most 0.022.
Values may be sent and summed in bfloat16 or wider, within the bound.
A program may use at most 64 MiB of HBM per device.

```python
import math
import jax
import jax.numpy as jnp
from jax import lax

D = 4096
F = 14336
BA = 128
BG = 896
POOL_DEV = 256
FGT_DEV = 64
RET_DEV = 32
NB = 32
NG = 16
POOL = 8192
FGT = 2048
RET = 1024


def place_ends(entries, key, low, top_value):
    extent = entries.shape
    spot = [jax.random.randint(jax.random.fold_in(key, axis), (), 0, extent[axis]) for axis in range(len(extent))]
    entries = entries.at[tuple(spot)].set(low)
    longest = extent.index(max(extent))
    spot[longest] = (spot[longest] + 1) % extent[longest]
    return entries.at[tuple(spot)].set(top_value)


def level_of(own_key, dims, shards, least, high):
    def one(position, parts):
        steps = jax.random.uniform(jax.random.fold_in(jax.random.fold_in(own_key, 6), position), (parts,), jnp.float32, least / len(shards), high / len(shards))
        return jnp.repeat(jnp.exp(steps), dims[position] // parts).reshape((-1,) + (1,) * (len(dims) - position - 1))

    loudness = one(*shards[0])
    for cut in shards[1:]:
        loudness = loudness * one(*cut)
    return loudness


def noise(stream_key, extent, deviation, reach, shards=(), held_as=jnp.bfloat16):
    values = deviation * jax.random.normal(stream_key, extent, jnp.float32)
    if shards:
        values = values * level_of(stream_key, extent, shards, -0.22, 0.18)
    return jnp.clip(values, -reach, reach).astype(held_as)


def setup_inputs(seed: int = 0) -> dict:
    keys = jax.random.split(jax.random.key(seed), 10)
    acts = noise(keys[0], (POOL, D), 1.0, 6.0, ((0, 32),))
    cots = noise(keys[1], (POOL, F), 1.0, 6.0, ((0, 32), (1, 16)))
    weight = noise(keys[2], (D, F), D ** -0.5, 0.09375, ((0, 32), (1, 16)))
    basis_in = noise(keys[3], (NB, BA, BA), BA ** -0.5, 0.5, ((0, 32),))
    basis_out = noise(keys[4], (NG, BG, BG), BG ** -0.5, 0.1875, ((0, 16), (1, 32)))
    eigen_in = jnp.clip(jnp.exp(math.log(5.0) - 3.218876 * jax.random.uniform(keys[5], (D,), jnp.float32) ** level_of(keys[5], (D,), ((0, 32),), -0.2, 0.2)), 0.2, 5.0)
    eigen_out = jnp.clip(jnp.exp(math.log(5.0) - 3.218876 * jax.random.uniform(keys[6], (F,), jnp.float32) ** level_of(keys[6], (F,), ((0, 16),), -0.2, 0.2)), 0.2, 5.0)
    forget_rows = place_ends(jax.random.randint(keys[7], (FGT,), 0, POOL_DEV), jax.random.fold_in(keys[7], 1), 0, POOL_DEV - 1).astype(jnp.int32)
    retain_rows = place_ends(jax.random.randint(keys[8], (RET,), 0, POOL_DEV), jax.random.fold_in(keys[8], 1), 0, POOL_DEV - 1).astype(jnp.int32)
    return dict(acts=acts, cots=cots, weight=weight, basis_in=basis_in, basis_out=basis_out, eigen_in=eigen_in, eigen_out=eigen_out, forget_rows=forget_rows, retain_rows=retain_rows)


damping = 0.1
step_size = 0.5


def reference(acts, cots, weight, basis_in, basis_out, eigen_in, eigen_out, forget_rows, retain_rows):
    forget_count = forget_rows.shape[0]
    retain_count = retain_rows.shape[0]
    forget_index = (jnp.arange(forget_count, dtype=jnp.int32) // FGT_DEV) * POOL_DEV + forget_rows.astype(jnp.int32)
    retain_index = (jnp.arange(retain_count, dtype=jnp.int32) // RET_DEV) * POOL_DEV + retain_rows.astype(jnp.int32)
    forget_acts = acts[forget_index]
    forget_cots = cots[forget_index]
    rotated_acts = jnp.einsum("tbi,bij->tbj", forget_acts.reshape(forget_count, NB, BA).astype(jnp.float32),
                              basis_in.astype(jnp.float32)).reshape(forget_count, D).astype(jnp.bfloat16)
    rotated_cots = jnp.einsum("tgi,gij->tgj", forget_cots.reshape(forget_count, NG, BG).astype(jnp.float32),
                              basis_out.astype(jnp.float32)).reshape(forget_count, F).astype(jnp.bfloat16)

    def column_block(column):
        offset = column * BG
        cot_block = lax.dynamic_slice_in_dim(rotated_cots, offset, BG, 1)
        moments = lax.dot_general(rotated_acts, cot_block, (((0,), (0,)), ((), ())),
                                  preferred_element_type=jnp.float32) / forget_count
        damped = eigen_in[:, None] * lax.dynamic_slice_in_dim(eigen_out, offset, BG, 0)[None, :] + damping
        scaled = (moments / damped).astype(jnp.bfloat16)
        block_basis = lax.dynamic_index_in_dim(basis_out, column, 0, keepdims=False)
        back_out = jnp.dot(scaled, block_basis.T, preferred_element_type=jnp.float32).astype(jnp.bfloat16)
        update = jnp.einsum("bij,bjc->bic", basis_in.astype(jnp.float32),
                            back_out.reshape(NB, BA, BG).astype(jnp.float32)).reshape(D, BG)
        old_block = lax.dynamic_slice_in_dim(weight, offset, BG, 1)
        return (old_block.astype(jnp.float32) + step_size * update).astype(jnp.bfloat16)

    blocks = lax.map(column_block, jnp.arange(NG, dtype=jnp.int32))
    new_weight = jnp.transpose(blocks, (1, 0, 2)).reshape(D, F)
    retain_acts = acts[retain_index]
    retain_cots = cots[retain_index]
    retained = jnp.dot(retain_acts, new_weight, preferred_element_type=jnp.float32).astype(jnp.bfloat16)
    back_grads = jnp.dot(retain_cots, new_weight.T, preferred_element_type=jnp.float32).astype(jnp.bfloat16)
    return (retained, back_grads)
```

```python
import functools

import jax
import jax.numpy as jnp
from jax import lax
from jax.experimental import pallas as pl
from jax.experimental.pallas import tpu as pltpu
from jax.sharding import PartitionSpec as P

damping = 0.1
step_size = 0.5
MESH = pl.DeviceIdType.MESH
BF = jnp.bfloat16
F32 = jnp.float32
NY, NH, NX, NC = 8, 4, 4, 4


def dot(a, b, ca, cb):
    return lax.dot_general(a, b, (((ca,), (cb,)), ((), ())), preferred_element_type=F32)


def body(fc, rc, cols, dblk, brows, forget_count,
         acts, cots, weight, basis_in, basis_out, eigen_in, eigen_out, frow, rrow,
         out_r, out_g,
         af, ar, asf, asr, cf, cr, bz, b112, bb, ts, tr, nw, rs, rr, gs, gr, g2, g3, go,
         ssem, rsem):
    f = lax.axis_index("fsdp")
    t = lax.axis_index("tp")
    y, h = f // NH, f % NH
    x, c = t // NC, t % NC

    def ydev(k):
        return (((y + k) % NY) * NH + h, t)

    def hdev(k):
        return (y * NH + (h + k) % NH, t)

    def tdev(k):
        return (f, (t + k) % 16)

    ypeers = [ydev(k) for k in range(1, NY)]
    hpeers = [hdev(k) for k in range(1, NH)]
    tpeers = [tdev(k) for k in range(1, 16)]
    bar = pltpu.get_barrier_semaphore()
    for p in ypeers + hpeers + tpeers:
        pl.semaphore_signal(bar, inc=1, device_id=p, device_id_type=MESH)

    count = [0]

    def sems(n):
        i = count[0]
        count[0] += n
        return i

    def rcopy(src, dst, i, dev):
        return pltpu.make_async_remote_copy(
            src_ref=src, dst_ref=dst, send_sem=ssem.at[i], recv_sem=rsem.at[i],
            device_id=dev, device_id_type=MESH)

    def rows_of(slot, n):
        return pl.ds(pl.multiple_of(slot * n, 16), n)

    pending = []

    class Ring:
        def __init__(self, buf, rows, cut):
            self.buf, self.rows, self.cut = buf, rows, cut
            self.base = sems(8)
            self.cps = [[], []]

        def send(self, s):
            for d in range(2):
                if s:
                    self.cps[d][s - 1].wait_recv()
                slot = (y - s) % NY if d == 0 else (y + s) % NY
                if s == 3:
                    lo, n = (0, self.cut) if d == 0 else (self.cut, self.rows - self.cut)
                else:
                    lo, n = 0, self.rows
                sl = pl.ds(pl.multiple_of(slot * self.rows + lo, 16), n)
                cp = rcopy(self.buf.at[sl], self.buf.at[sl], self.base + d * 4 + s, ydev(1 if d == 0 else NY - 1))
                cp.start()
                self.cps[d].append(cp)
                pending.append(cp)

        def finish(self):
            for d in range(2):
                self.cps[d][3].wait_recv()

    pool = acts.shape[0]
    ohf = (lax.broadcasted_iota(jnp.int32, (pool, fc), 0) == frow[...]).astype(BF)
    ohr = (lax.broadcasted_iota(jnp.int32, (pool, rc), 0) == rrow[...]).astype(BF)
    cf[rows_of(y, fc), :] = dot(ohf, cots[...], 0, 0).astype(BF)
    bz[pl.ds(pl.multiple_of(h * 32, 16), 32), :] = jnp.zeros((32, cols), BF)
    bz[pl.ds(pl.multiple_of(h * 32, 16), brows), :] = basis_out[0]

    pl.semaphore_wait(bar, len(ypeers) + len(hpeers) + len(tpeers))

    ring_cf = Ring(cf, fc, fc // 2)
    ring_cf.send(0)

    ib = sems(3)
    bcps = []
    for k in range(1, NH):
        sl = pl.ds(pl.multiple_of(h * 32, 16), 32)
        cp = rcopy(bz.at[sl], bz.at[sl], ib + k - 1, hdev(k))
        cp.start()
        bcps.append(cp)
        pending.append(cp)

    for j in range(NY):
        asf[j] = dot(ohf, acts[:, j * dblk:(j + 1) * dblk], 0, 0).astype(BF)
    ia = sems(7)
    acps = []
    for k in (1, 7, 2, 6, 3, 5, 4):
        cp = rcopy(asf.at[(y + k) % NY], af.at[rows_of(y, fc)], ia + k - 1, ydev(k))
        cp.start()
        acps.append(cp)
        pending.append(cp)
    af[rows_of(y, fc), :] = asf[y]

    ring_cf.send(1)
    cr[rows_of(y, rc), :] = dot(ohr, cots[...], 0, 0).astype(BF)
    for j in range(NY):
        asr[j] = dot(ohr, acts[:, j * dblk:(j + 1) * dblk], 0, 0).astype(BF)
    ring_cf.send(2)
    ring_cf.send(3)

    for cp in bcps:
        cp.wait_recv()
    parts = [bz[k * 32:k * 32 + brows, :].astype(F32) for k in range(NH)]
    b112[...] = jnp.concatenate(parts, axis=0)
    bb[rows_of(y, NH * brows), :] = b112[...].astype(BF)
    ring_b = Ring(bb, NH * brows, 64)
    ring_b.send(0)

    for cp in acps:
        cp.wait_recv()
    ring_cf.finish()

    for q in range(NH):
        ts[q] = dot(af[:, q * 128:(q + 1) * 128], cf[...], 0, 0).astype(BF)
    it = sems(3)
    tcps = []
    for k in (1, 3, 2):
        cp = rcopy(ts.at[(h + k) % NH], tr.at[k - 1], it + k - 1, hdev(k))
        cp.start()
        tcps.append(cp)
        pending.append(cp)

    ring_b.send(1)
    ring_cr = Ring(cr, rc, rc // 2)
    ring_cr.send(0)
    ia = sems(7)
    rcps = []
    for k in (1, 7, 2, 6, 3, 5, 4):
        cp = rcopy(asr.at[(y + k) % NY], ar.at[rows_of(y, rc)], ia + k - 1, ydev(k))
        cp.start()
        rcps.append(cp)
        pending.append(cp)
    ar[rows_of(y, rc), :] = asr[y]
    ring_b.send(2)
    ring_cr.send(1)
    ring_b.send(3)
    ring_cr.send(2)
    ring_cr.send(3)

    for cp in tcps:
        cp.wait_recv()
    mom = ts[h].astype(F32) + tr[0].astype(F32) + tr[1].astype(F32) + tr[2].astype(F32)
    q_in = basis_in[0]
    rot = dot(q_in, mom.astype(BF), 0, 0).astype(BF)
    ring_b.finish()
    m2 = dot(rot, bb[...], 1, 0) / forget_count
    eye = lax.broadcasted_iota(jnp.int32, (128, 128), 0) == lax.broadcasted_iota(jnp.int32, (128, 128), 1)
    ein = jnp.sum(jnp.where(eye, eigen_in[...], 0.0), axis=1, keepdims=True)
    scaled = (m2 / (ein * eigen_out[...] + damping)).astype(BF)
    back = dot(scaled, bb[...], 1, 1).astype(BF)
    upd = dot(q_in, back, 1, 0)
    nw[rows_of(h, 128), :] = (weight[...].astype(F32) + step_size * upd).astype(BF)

    iw = sems(3)
    wcps = []
    for k in (1, 3, 2):
        cp = rcopy(nw.at[rows_of(h, 128)], nw.at[rows_of(h, 128)], iw + k - 1, hdev(k))
        cp.start()
        wcps.append(cp)
        pending.append(cp)
    for cp in rcps:
        cp.wait_recv()
    ring_cr.finish()
    for cp in wcps:
        cp.wait_recv()

    for q in range(NH):
        g = dot(cr[...], nw[q * 128:(q + 1) * 128, :], 1, 1)
        for r in range(NC):
            gs[q * NC + r] = g[r * 64:(r + 1) * 64, :].astype(BF)
    ig = sems(15)
    gcps = []
    for k in range(1, 16):
        cp = rcopy(gs.at[(t + k) % 16], gr.at[k - 1], ig + k - 1, tdev(k))
        cp.start()
        gcps.append(cp)
        pending.append(cp)

    for j in range(NY):
        rs[j] = dot(ar[j * rc:(j + 1) * rc, :], nw[...], 1, 0).astype(BF)
    ir = sems(7)
    scps = []
    for k in (1, 7, 2, 6, 3, 5, 4):
        cp = rcopy(rs.at[(y + k) % NY], rr.at[k - 1], ir + k - 1, ydev(k))
        cp.start()
        scps.append(cp)
        pending.append(cp)

    for cp in gcps:
        cp.wait_recv()
    tot = gs[t].astype(F32)
    for k in range(15):
        tot = tot + gr[k].astype(F32)
    g2[...] = tot.astype(BF)

    i2 = sems(8)
    s2 = sems(2)
    for i in range(2):
        yo = 2 * c + i
        k = (yo - y) % NY

        def copy2():
            return pltpu.make_async_remote_copy(
                src_ref=g2.at[pl.ds(i * rc, rc)], dst_ref=g3.at[y],
                send_sem=ssem.at[s2 + i], recv_sem=rsem.at[i2 + k],
                device_id=(yo * NH + h, t), device_id_type=MESH)

        @pl.when(k != 0)
        def _():
            copy2().start()

        @pl.when(k == 0)
        def _():
            g3[y] = g2[i * rc:(i + 1) * rc, :]

    i3 = sems(4)
    s3 = sems(15)
    mine = (y // 2) == c

    @pl.when(mine)
    def _():
        for k in range(1, NY):
            rcopy(g2.at[pl.ds(0, rc)], g3.at[y], i2 + k, ydev(k)).wait_recv()
        for k in range(1, 16):
            pltpu.make_async_remote_copy(
                src_ref=g3, dst_ref=go.at[x], send_sem=ssem.at[s3 + k - 1],
                recv_sem=rsem.at[i3 + x], device_id=tdev(k), device_id_type=MESH).start()
        go[x] = g3[...]

    for cp in scps:
        cp.wait_recv()
    tot = rs[y].astype(F32)
    for k in range(7):
        tot = tot + rr[k].astype(F32)
    out_r[...] = tot.astype(BF)

    for i in range(2):
        yo = 2 * c + i

        @pl.when(yo != y)
        def _():
            pltpu.make_async_remote_copy(
                src_ref=g2.at[pl.ds(i * rc, rc)], dst_ref=g3.at[y],
                send_sem=ssem.at[s2 + i], recv_sem=rsem.at[i2],
                device_id=(yo * NH + h, t), device_id_type=MESH).wait_send()

    for xs in range(NX):
        @pl.when(jnp.logical_not(jnp.logical_and(mine, x == xs)))
        def _():
            pltpu.make_async_remote_copy(
                src_ref=g3, dst_ref=go.at[xs], send_sem=ssem.at[s3],
                recv_sem=rsem.at[i3 + xs], device_id=tdev(1), device_id_type=MESH).wait_recv()
    for q in range(NX):
        for j in range(NY):
            lo = j * dblk + q * 128
            out_g[:, lo:lo + 128] = go[q, j]

    @pl.when(mine)
    def _():
        for k in range(1, 16):
            pltpu.make_async_remote_copy(
                src_ref=g3, dst_ref=go.at[x], send_sem=ssem.at[s3 + k - 1],
                recv_sem=rsem.at[i3], device_id=tdev(k), device_id_type=MESH).wait_send()
    for cp in pending:
        cp.wait_send()
    assert count[0] <= 120


def shards(acts, cots, weight, basis_in, basis_out, eigen_in, eigen_out, forget_rows, retain_rows):
    fc, rc = forget_rows.shape[0], retain_rows.shape[0]
    cols = cots.shape[1]
    dim = acts.shape[1]
    dblk = dim // NY
    brows = basis_out.shape[1]
    vm = lambda *s: pltpu.VMEM(s, BF)
    kern = functools.partial(body, fc, rc, cols, dblk, brows, float(fc * NY * NH))
    return pl.pallas_call(
        kern,
        out_shape=(jax.ShapeDtypeStruct((rc, cols), BF), jax.ShapeDtypeStruct((rc, dim), BF)),
        in_specs=[pl.BlockSpec(memory_space=pltpu.VMEM)] * 9,
        out_specs=(pl.BlockSpec(memory_space=pltpu.VMEM),) * 2,
        scratch_shapes=[
            vm(NY * fc, dblk), vm(NY * rc, dblk), vm(NY, fc, dblk), vm(NY, rc, dblk),
            vm(NY * fc, cols), vm(NY * rc, cols),
            vm(NH * 32, cols), pltpu.VMEM((NH * brows, cols), F32), vm(cols, cols),
            vm(NH, 128, cols), vm(NH - 1, 128, cols), vm(NH * 128, cols),
            vm(NY, rc, cols), vm(NY - 1, rc, cols),
            vm(16, 64, 128), vm(15, 64, 128), vm(64, 128), vm(NY, rc, 128), vm(NX, NY, rc, 128),
            pltpu.SemaphoreType.DMA((120,)), pltpu.SemaphoreType.DMA((120,)),
        ],
        compiler_params=pltpu.CompilerParams(collective_id=0, has_side_effects=True, vmem_limit_bytes=50 * 2**20),
        name="newton_step",
    )(acts, cots, weight, basis_in, basis_out, eigen_in.reshape(1, -1), eigen_out.reshape(1, -1),
      forget_rows.reshape(1, -1), retain_rows.reshape(1, -1))


def solution(mesh):
    placed = (
        P("fsdp", None),
        P("fsdp", "tp"),
        P("fsdp", "tp"),
        P("fsdp", None, None),
        P("tp", "fsdp", None),
        P("fsdp"),
        P("tp"),
        P("fsdp"),
        P("fsdp"),
    )
    return jax.shard_map(
        shards,
        mesh=mesh,
        in_specs=placed,
        out_specs=(P("fsdp", "tp"), P("fsdp", None)),
        check_vma=False,
    )
```

```python
import functools

import jax
import jax.numpy as jnp
from jax import lax
from jax.experimental import pallas as pl
from jax.experimental.pallas import tpu as pltpu
from jax.sharding import PartitionSpec as P

damping = 0.1
step_size = 0.5
MESH = pl.DeviceIdType.MESH
BF = jnp.bfloat16
F32 = jnp.float32
NY, NH, NX, NC = 8, 4, 4, 4
NSEM = 200


def dot(a, b, ca, cb):
    return lax.dot_general(a, b, (((ca,), (cb,)), ((), ())), preferred_element_type=F32)


def body(fc, rc, cols, dblk, brows, forget_count,
         acts_in, cots_in, weight_in, basis_in_in, basis_out_in, eigen_in_in, eigen_out_in, frow_in, rrow_in,
         out_r, out_g,
         acb, cots, weight, basis_in, bsrc, ein_v, eout_v, frow, rrow,
         af, ar, asf, asr, cf, cr, bz, b112, bb, ts, tf, tg, tr, nw, rs, rr, gs, gr, g2, g3, go,
         lsem, ssem, rsem):
    f = lax.axis_index("fsdp")
    t = lax.axis_index("tp")
    y, h = f // NH, f % NH
    x, c = t // NC, t % NC
    half, core = c // 2, c % 2

    def dev(h_, x_, c_):
        return (y * NH + h_, x_ * NC + c_)

    def ydev(k):
        return (((y + k) % NY) * NH + h, t)

    def hdev(k):
        return dev((h + k) % NH, x, c)

    def tdev(k):
        return (f, (t + k) % 16)

    loads = []

    def load(src, dst):
        cp = pltpu.make_async_copy(src, dst, lsem.at[len(loads)])
        cp.start()
        loads.append(cp)
        return cp

    l_fr = load(frow_in, frow)
    l_rr = load(rrow_in, rrow)
    l_cots = load(cots_in, cots)
    l_acts = [load(acts_in.at[:, pl.ds(pl.multiple_of(j * dblk + x * 128, 128), 128)], acb.at[:, j * 128:(j + 1) * 128])
              for j in range(NY)]
    l_b = load(basis_out_in, bsrc)
    l_w = load(weight_in, weight)
    l_q = load(basis_in_in, basis_in)
    l_ein = load(eigen_in_in, ein_v)
    l_eout = load(eigen_out_in, eout_v)

    bar = pltpu.get_barrier_semaphore()
    peers = [ydev(k) for k in range(1, NY)] + [hdev(k) for k in range(1, NH)] + [tdev(k) for k in range(1, 16)]
    for p in peers:
        pl.semaphore_signal(bar, inc=1, device_id=p, device_id_type=MESH)

    count = [0]

    def sems(n):
        i = count[0]
        count[0] += n
        return i

    def rcopy(src, dst, i, to):
        return pltpu.make_async_remote_copy(
            src_ref=src, dst_ref=dst, send_sem=ssem.at[i], recv_sem=rsem.at[i],
            device_id=to, device_id_type=MESH)

    pending = []

    def push(src, dst, i, to):
        cp = rcopy(src, dst, i, to)
        cp.start()
        pending.append(cp)
        return cp

    def rows_of(slot, n):
        return pl.ds(pl.multiple_of(slot * n, 16), n)

    class Ring:
        def __init__(self, buf, stride, first, rows, part):
            self.buf, self.stride, self.first, self.rows, self.part = buf, stride, first, rows, part
            self.base = sems(8)
            self.cps = [[], []]

        def send(self, s):
            for d in range(2):
                if s:
                    self.cps[d][s - 1].wait_recv()
                slot = (y - s) % NY if d == 0 else (y + s) % NY
                lo, n = self.first, self.rows
                if s == 3:
                    lo, n = (lo, self.part) if d == 0 else (lo + self.part, n - self.part)
                sl = pl.ds(pl.multiple_of(slot * self.stride + lo, 16), n)
                self.cps[d].append(push(self.buf.at[sl], self.buf.at[sl], self.base + d * 4 + s,
                                        ydev(1 if d == 0 else NY - 1)))

        def finish(self):
            for d in range(2):
                self.cps[d][3].wait_recv()

    pool = acb.shape[0]
    l_fr.wait()
    l_rr.wait()
    ohf = (lax.broadcasted_iota(jnp.int32, (pool, fc), 0) == frow[...]).astype(BF)
    ohr = (lax.broadcasted_iota(jnp.int32, (pool, rc), 0) == rrow[...]).astype(BF)
    l_cots.wait()
    cf[rows_of(y, fc), :] = dot(ohf, cots[...], 0, 0).astype(BF)
    for cp in l_acts:
        cp.wait()
    sel = dot(ohf, acb[...], 0, 0).astype(BF)
    for j in range(NY):
        asf[j] = sel[:, j * 128:(j + 1) * 128]
    l_b.wait()
    mine_b = rows_of(h, 32)
    bz[mine_b, :] = jnp.zeros((32, cols), BF)
    bz[pl.ds(pl.multiple_of(h * 32, 16), brows), :] = bsrc[0]
    pl.semaphore_wait(bar, len(peers))

    rings_cf = [Ring(cf, fc, 0, fc // 2, fc // 4), Ring(cf, fc, fc // 2, fc // 2, fc // 4)]
    for r in rings_cf:
        r.send(0)
    i = sems(8)
    p_af = [push(asf.at[(y + k) % NY], af.at[x, rows_of(y, fc)], i + k, ydev(k)) for k in (1, 7, 2, 6, 3, 5, 4)]
    af[x, rows_of(y, fc), :] = asf[y]
    i = sems(3)
    g_b = [push(bz.at[mine_b], bz.at[mine_b], i + k - 1, hdev(k)) for k in (1, 3, 2)]
    for r in rings_cf:
        r.send(1)
    for cp in p_af:
        cp.wait_recv()
    i = sems(3)
    g_af = [push(af.at[x], af.at[x], i + k - 1, dev(h, (x + k) % NX, c)) for k in (1, 3, 2)]
    for r in rings_cf:
        r.send(2)
    cr[rows_of(y, rc), :] = dot(ohr, cots[...], 0, 0).astype(BF)
    sel = dot(ohr, acb[...], 0, 0).astype(BF)
    for j in range(NY):
        asr[j] = sel[:, j * 128:(j + 1) * 128]
    for r in rings_cf:
        r.send(3)

    for cp in g_b:
        cp.wait_recv()
    b112[...] = jnp.concatenate([bz[k * 32:k * 32 + brows, :].astype(F32) for k in range(NH)], axis=0)
    bb[rows_of(y, NH * brows), :] = b112[...].astype(BF)
    ring_b = Ring(bb, NH * brows, 0, NH * brows, 64)
    ring_b.send(0)

    for cp in g_af:
        cp.wait_recv()
    for r in rings_cf:
        r.finish()

    up, down, far = (h + 1) % NH, (h + 3) % NH, (h + 2) % NH
    for k, q in enumerate((far, up, down, h)):
        ts[q] = dot(af[q], cf[...], 0, 0).astype(BF)
        if k == 0:
            i = sems(6)
            far_up = push(ts.at[far, 0:64], tf.at[0], i, hdev(1))
            far_down = push(ts.at[far, 64:128], tf.at[1], i + 1, hdev(3))
        if k == 1:
            plain_up = push(ts.at[up, 64:128], tr.at[0, 64:128], i + 2, hdev(1))
        if k == 2:
            plain_down = push(ts.at[down, 0:64], tr.at[1, 0:64], i + 3, hdev(3))
    ring_b.send(1)
    far_up.wait_recv()
    tg[0] = (tf[0].astype(F32) + ts[up, 0:64].astype(F32)).astype(BF)
    both_up = push(tg.at[0], tr.at[0, 0:64], i + 4, hdev(1))
    far_down.wait_recv()
    tg[1] = (tf[1].astype(F32) + ts[down, 64:128].astype(F32)).astype(BF)
    both_down = push(tg.at[1], tr.at[1, 64:128], i + 5, hdev(3))

    i = sems(8)
    p_ar = [push(asr.at[(y + k) % NY], ar.at[x, rows_of(y, rc)], i + k, ydev(k)) for k in (1, 7, 2, 6, 3, 5, 4)]
    ar[x, rows_of(y, rc), :] = asr[y]
    ring_b.send(2)
    ring_b.send(3)
    ring_cr = Ring(cr, rc, 0, rc, rc // 2)
    ring_cr.send(0)
    for cp in p_ar:
        cp.wait_recv()
    i = sems(3)
    g_ar = [push(ar.at[x], ar.at[x], i + k - 1, dev(h, (x + k) % NX, c)) for k in (1, 3, 2)]

    for cp in (plain_up, plain_down, both_up, both_down):
        cp.wait_recv()
    mom = ts[h].astype(F32) + tr[0].astype(F32) + tr[1].astype(F32)
    l_q.wait()
    q_in = basis_in[0]
    rot = dot(q_in, mom.astype(BF), 0, 0).astype(BF)
    ring_cr.send(1)
    ring_b.finish()
    m2 = dot(rot, bb[...], 1, 0) / forget_count
    eye = lax.broadcasted_iota(jnp.int32, (128, 128), 0) == lax.broadcasted_iota(jnp.int32, (128, 128), 1)
    l_ein.wait()
    l_eout.wait()
    ein = jnp.sum(jnp.where(eye, ein_v[...], 0.0), axis=1, keepdims=True)
    scaled = (m2 / (ein * eout_v[...] + damping)).astype(BF)
    l_w.wait()

    parts = ((0, 512), (512, cols - 512))
    own, fwd = [], [None, None]
    ig = [sems(6), sems(6)]
    for p, (lo, n) in enumerate(parts):
        cs = pl.ds(lo, n)
        back = dot(scaled, bb[lo:lo + n, :], 1, 1).astype(BF)
        upd = dot(q_in, back, 1, 0)
        nw[h, :, lo:lo + n] = (weight[:, lo:lo + n].astype(F32) + step_size * upd).astype(BF)
        a, b = nw.at[h, 0:64, cs], nw.at[h, 64:128, cs]
        own.append([push(a, a, ig[p], hdev(1)), push(b, b, ig[p] + 1, hdev(3)),
                    push(b, b, ig[p] + 2, hdev(1)), push(a, a, ig[p] + 3, hdev(3))])

    def forward(p):
        cs = pl.ds(parts[p][0], parts[p][1])
        own[p][0].wait_recv()
        a = nw.at[down, 0:64, cs]
        one = push(a, a, ig[p] + 4, hdev(1))
        own[p][1].wait_recv()
        b = nw.at[up, 64:128, cs]
        fwd[p] = (one, push(b, b, ig[p] + 5, hdev(3)))

    igr = sems(16)

    def gradients(q):
        g = dot(cr[...], nw[q], 1, 1)
        for s in range(2):
            for p in range(2):
                ct = 2 * s + p
                gs[q * NC + ct] = jnp.concatenate(
                    [g[(4 * p + i) * rc + 16 * s:(4 * p + i) * rc + 16 * s + 16, :] for i in range(4)], axis=0).astype(BF)
                e = (q * NC + ct - t) % 16
                cp = rcopy(gs.at[q * NC + ct], gr.at[e], igr + e, dev(h, q, ct))

                @pl.when(e != 0)
                def _():
                    cp.start()

    p_r = []

    def retained(p):
        lo, n = parts[p]
        tot = dot(ar[0], nw[0, :, lo:lo + n], 1, 0)
        for q in range(1, NH):
            tot = tot + dot(ar[q], nw[q, :, lo:lo + n], 1, 0)
        for j in range(NY):
            rs[j, :, lo:lo + n] = tot[j * rc:(j + 1) * rc, :].astype(BF)
        i = sems(8)
        cs = pl.ds(lo, n)
        for k in (1, 7, 2, 6, 3, 5, 4):
            p_r.append(push(rs.at[(y + k) % NY, :, cs], rr.at[k, :, cs], i + k, ydev(k)))

    ring_cr.send(2)
    forward(0)
    ring_cr.send(3)
    for cp in g_ar:
        cp.wait_recv()
    ring_cr.finish()
    gradients(h)
    forward(1)
    for cp in (own[0][2], own[0][3]) + fwd[0]:
        cp.wait_recv()
    retained(0)
    for cp in (own[1][2], own[1][3]):
        cp.wait_recv()
    gradients(up)
    gradients(down)
    for cp in fwd[1]:
        cp.wait_recv()
    gradients(far)
    retained(1)

    gsum = gs[t].astype(F32)
    for e in range(1, 16):
        rcopy(gs.at[0], gr.at[e], igr + e, ydev(1)).wait_recv()
        gsum = gsum + gr[e].astype(F32)
    g2[...] = gsum.astype(BF)

    i2 = sems(8)
    s2 = sems(4)

    def own_part(i):
        yo = 4 * core + i
        k = (yo - y) % NY
        return k, pltpu.make_async_remote_copy(
            src_ref=g2.at[i * 16:(i + 1) * 16], dst_ref=g3.at[y], send_sem=ssem.at[s2 + i], recv_sem=rsem.at[i2 + k],
            device_id=(yo * NH + h, t), device_id_type=MESH)

    for i in range(4):
        k, cp = own_part(i)

        @pl.when(k != 0)
        def _():
            cp.start()

        @pl.when(k == 0)
        def _():
            g3[y] = g2[i * 16:(i + 1) * 16, :]

    i3 = sems(8)
    s3 = sems(16)
    mine = (y // 4) == core

    def final(k):
        return pltpu.make_async_remote_copy(
            src_ref=g3, dst_ref=go.at[2 * x + half], send_sem=ssem.at[s3 + k], recv_sem=rsem.at[i3 + 2 * x + half],
            device_id=tdev(k), device_id_type=MESH)

    @pl.when(mine)
    def _():
        for k in range(1, NY):
            rcopy(g2.at[0:16], g3.at[y], i2 + k, ydev(1)).wait_recv()
        for k in (1, 15, 2, 14, 3, 13, 4, 12, 5, 11, 6, 10, 7, 9, 8):
            final(k).start()
        go[2 * x + half] = g3[...]

    for cp in p_r:
        cp.wait_recv()
    tot = rs[y].astype(F32)
    for k in range(1, NY):
        tot = tot + rr[k].astype(F32)
    out_r[...] = tot.astype(BF)

    for cp in pending:
        cp.wait_send()
    for e in range(1, 16):
        rcopy(gs.at[0], gr.at[e], igr + e, ydev(1)).wait_send()
    for i in range(4):
        k, cp = own_part(i)

        @pl.when(k != 0)
        def _():
            cp.wait_send()

    for q in range(NX):
        for s in range(2):
            @pl.when(jnp.logical_not(jnp.logical_and(mine, 2 * x + half == 2 * q + s)))
            def _():
                rcopy(g3, go.at[2 * q + s], i3 + 2 * q + s, ydev(1)).wait_recv()
            for j in range(NY):
                lo = j * dblk + q * 128
                out_g[16 * s:16 * s + 16, lo:lo + 128] = go[2 * q + s, j]

    @pl.when(mine)
    def _():
        for k in range(1, 16):
            final(k).wait_send()
    assert count[0] <= NSEM


def shards(acts, cots, weight, basis_in, basis_out, eigen_in, eigen_out, forget_rows, retain_rows):
    fc, rc = forget_rows.shape[0], retain_rows.shape[0]
    pool, cols = cots.shape
    dim = acts.shape[1]
    dblk = dim // NY
    brows = basis_out.shape[1]
    vm = lambda *s: pltpu.VMEM(s, BF)
    vf = lambda *s: pltpu.VMEM(s, F32)
    kern = functools.partial(body, fc, rc, cols, dblk, brows, float(fc * NY * NH))
    return pl.pallas_call(
        kern,
        out_shape=(jax.ShapeDtypeStruct((rc, cols), BF), jax.ShapeDtypeStruct((rc, dim), BF)),
        in_specs=[pl.BlockSpec(memory_space=pl.ANY)] * 9,
        out_specs=(pl.BlockSpec(memory_space=pltpu.VMEM),) * 2,
        scratch_shapes=[
            vm(pool, NY * 128), vm(pool, cols), vm(128, cols), vm(1, 128, 128), vm(1, brows, cols),
            vf(1, 128), vf(1, cols), pltpu.VMEM((1, fc), jnp.int32), pltpu.VMEM((1, rc), jnp.int32),
            vm(NH, NY * fc, 128), vm(NH, NY * rc, 128), vm(NY, fc, 128), vm(NY, rc, 128),
            vm(NY * fc, cols), vm(NY * rc, cols),
            vm(NH * 32, cols), vf(NH * brows, cols), vm(cols, cols),
            vm(NH, 128, cols), vm(2, 64, cols), vm(2, 64, cols), vm(2, 128, cols), vm(NH, 128, cols),
            vm(NY, rc, cols), vm(NY, rc, cols),
            vm(16, 64, 128), vm(16, 64, 128), vm(64, 128), vm(NY, 16, 128), vm(2 * NX, NY, 16, 128),
            pltpu.SemaphoreType.DMA((20,)), pltpu.SemaphoreType.DMA((NSEM,)), pltpu.SemaphoreType.DMA((NSEM,)),
        ],
        compiler_params=pltpu.CompilerParams(collective_id=0, has_side_effects=True, vmem_limit_bytes=62 * 2**20),
        name="newton_step",
    )(acts, cots, weight, basis_in, basis_out, eigen_in.reshape(1, -1), eigen_out.reshape(1, -1),
      forget_rows.reshape(1, -1), retain_rows.reshape(1, -1))


def solution(mesh):
    placed = (
        P("fsdp", None),
        P("fsdp", "tp"),
        P("fsdp", "tp"),
        P("fsdp", None, None),
        P("tp", "fsdp", None),
        P("fsdp"),
        P("tp"),
        P("fsdp"),
        P("fsdp"),
    )
    return jax.shard_map(
        shards,
        mesh=mesh,
        in_specs=placed,
        out_specs=(P("fsdp", "tp"), P("fsdp", None)),
        check_vma=False,
    )
```

```python
import functools

import jax
import jax.numpy as jnp
from jax import lax
from jax.experimental import pallas as pl
from jax.experimental.pallas import tpu as pltpu
from jax.sharding import PartitionSpec as P

damping = 0.1
step_size = 0.5
MESH = pl.DeviceIdType.MESH
BF = jnp.bfloat16
F32 = jnp.float32
NY, NH, NX, NC = 8, 4, 4, 4
NSEM = 200


def dot(a, b, ca, cb):
    return lax.dot_general(a, b, (((ca,), (cb,)), ((), ())), preferred_element_type=F32)


def body(fc, rc, cols, dblk, brows, forget_count,
         acts_in, cots_in, weight_in, basis_in_in, basis_out_in, eigen_in_in, eigen_out_in, frow_in, rrow_in,
         out_r, out_g,
         acb, cots, weight, basis_in, bsrc, ein_v, eout_v, frow, rrow,
         af, ar, asf, asr, cf, cr, bz, b112, bb, ts, tf, tg, tr, nw, rs, rr, gs, gr, g2, g3, go,
         lsem, ssem, rsem):
    f = lax.axis_index("fsdp")
    t = lax.axis_index("tp")
    y, h = f // NH, f % NH
    x, c = t // NC, t % NC
    half, core = c // 2, c % 2

    def dev(h_, x_, c_):
        return (y * NH + h_, x_ * NC + c_)

    def ydev(k):
        return (((y + k) % NY) * NH + h, t)

    def hdev(k):
        return dev((h + k) % NH, x, c)

    def tdev(k):
        return (f, (t + k) % 16)

    loads = []

    def load(src, dst):
        cp = pltpu.make_async_copy(src, dst, lsem.at[len(loads)])
        cp.start()
        loads.append(cp)
        return cp

    l_fr = load(frow_in, frow)
    l_rr = load(rrow_in, rrow)
    l_cots = load(cots_in, cots)
    l_acts = [load(acts_in.at[:, pl.ds(pl.multiple_of(j * dblk + x * 128, 128), 128)], acb.at[:, j * 128:(j + 1) * 128])
              for j in range(NY)]
    l_b = load(basis_out_in, bsrc)
    l_w = load(weight_in, weight)
    l_q = load(basis_in_in, basis_in)
    l_ein = load(eigen_in_in, ein_v)
    l_eout = load(eigen_out_in, eout_v)

    bar = pltpu.get_barrier_semaphore()
    peers = [ydev(k) for k in range(1, NY)] + [hdev(k) for k in range(1, NH)] + [tdev(k) for k in range(1, 16)]
    for p in peers:
        pl.semaphore_signal(bar, inc=1, device_id=p, device_id_type=MESH)

    count = [0]

    def sems(n):
        i = count[0]
        count[0] += n
        return i

    def rcopy(src, dst, i, to):
        return pltpu.make_async_remote_copy(
            src_ref=src, dst_ref=dst, send_sem=ssem.at[i], recv_sem=rsem.at[i],
            device_id=to, device_id_type=MESH)

    pending = []

    def push(src, dst, i, to):
        cp = rcopy(src, dst, i, to)
        cp.start()
        pending.append(cp)
        return cp

    def rows_of(slot, n):
        return pl.ds(pl.multiple_of(slot * n, 16), n)

    class Ring:
        def __init__(self, buf, rows, part, first=0, n=None, cs=None):
            self.buf, self.rows, self.part = buf, rows, part
            self.first, self.n = first, rows if n is None else n
            self.cs = pl.ds(0, cols) if cs is None else cs
            self.base = sems(8)
            self.cps = [[], []]

        def send(self, s):
            for d in range(2):
                if s:
                    self.cps[d][s - 1].wait_recv()
                slot = (y - s) % NY if d == 0 else (y + s) % NY
                lo, n = self.first, self.n
                if s == 3:
                    lo, n = (lo, self.part) if d == 0 else (lo + self.part, n - self.part)
                sl = self.buf.at[pl.ds(pl.multiple_of(slot * self.rows + lo, 16), n), self.cs]
                self.cps[d].append(push(sl, sl, self.base + d * 4 + s, ydev(1 if d == 0 else NY - 1)))

        def finish(self):
            for d in range(2):
                self.cps[d][3].wait_recv()

    pool = acb.shape[0]
    l_fr.wait()
    l_rr.wait()
    ohf = (lax.broadcasted_iota(jnp.int32, (pool, fc), 0) == frow[...]).astype(BF)
    ohr = (lax.broadcasted_iota(jnp.int32, (pool, rc), 0) == rrow[...]).astype(BF)
    l_cots.wait()
    cf[rows_of(y, fc), :] = dot(ohf, cots[...], 0, 0).astype(BF)
    for cp in l_acts:
        cp.wait()
    sel = dot(ohf, acb[...], 0, 0).astype(BF)
    for j in range(NY):
        asf[j] = sel[:, j * 128:(j + 1) * 128]
    l_b.wait()
    mine_b = rows_of(h, 32)
    bz[mine_b, :] = jnp.zeros((32, cols), BF)
    bz[pl.ds(pl.multiple_of(h * 32, 16), brows), :] = bsrc[0]
    pl.semaphore_wait(bar, len(peers))

    parts = ((0, 512), (512, cols - 512))
    i = sems(8)
    p_af = [push(asf.at[(y + k) % NY], af.at[x, rows_of(y, fc)], i + k, ydev(k)) for k in (1, 7, 2, 6, 3, 5, 4)]
    rings_cf = [Ring(cf, fc, fc // 2, cs=pl.ds(lo, n)) for lo, n in parts]
    for r in rings_cf:
        r.send(0)
    i = sems(3)
    g_b = [push(bz.at[mine_b], bz.at[mine_b], i + k - 1, hdev(k)) for k in (1, 3, 2)]
    af[x, rows_of(y, fc), :] = asf[y]
    sel = dot(ohr, acb[...], 0, 0).astype(BF)
    for j in range(NY):
        asr[j] = sel[:, j * 128:(j + 1) * 128]
    cr[rows_of(y, rc), :] = dot(ohr, cots[...], 0, 0).astype(BF)
    for cp in p_af:
        cp.wait_recv()
    i = sems(3)
    g_af = [push(af.at[x], af.at[x], i + k - 1, dev(h, (x + k) % NX, c)) for k in (1, 3, 2)]
    for r in rings_cf:
        r.send(1)
    i = sems(8)
    p_ar = [push(asr.at[(y + k) % NY], ar.at[x, rows_of(y, rc)], i + k, ydev(k)) for k in (1, 7, 2, 6, 3, 5, 4)]
    ring_cr = Ring(cr, rc, rc // 2)
    ring_cr.send(0)
    ar[x, rows_of(y, rc), :] = asr[y]
    for cp in g_b:
        cp.wait_recv()
    b112[...] = jnp.concatenate([bz[k * 32:k * 32 + brows, :].astype(F32) for k in range(NH)], axis=0)
    bb[rows_of(y, NH * brows), :] = b112[...].astype(BF)
    rings_b = [Ring(bb, NH * brows, 32, 0, 64), Ring(bb, NH * brows, 32, 64, NH * brows - 64)]
    for r in rings_cf:
        r.send(2)
    ring_cr.send(1)
    for r in rings_cf:
        r.send(3)
    for r in rings_b:
        r.send(0)
    for cp in p_ar:
        cp.wait_recv()
    i = sems(3)
    for cp in g_af:
        cp.wait_recv()
    g_ar = [push(ar.at[x], ar.at[x], i + k - 1, dev(h, (x + k) % NX, c)) for k in (1, 3, 2)]

    up, down, far = (h + 1) % NH, (h + 3) % NH, (h + 2) % NH
    its, first = [], []
    for p, (lo, n) in enumerate(parts):
        cs = pl.ds(lo, n)
        rings_cf[p].finish()
        i = sems(6)
        its.append(i)
        ts[far, :, lo:lo + n] = dot(af[far], cf[:, lo:lo + n], 0, 0).astype(BF)
        far_up = push(ts.at[far, 0:64, cs], tf.at[0, :, cs], i, hdev(1))
        far_down = push(ts.at[far, 64:128, cs], tf.at[1, :, cs], i + 1, hdev(3))
        ts[up, :, lo:lo + n] = dot(af[up], cf[:, lo:lo + n], 0, 0).astype(BF)
        plain_up = push(ts.at[up, 64:128, cs], tr.at[0, 64:128, cs], i + 2, hdev(1))
        ts[down, :, lo:lo + n] = dot(af[down], cf[:, lo:lo + n], 0, 0).astype(BF)
        plain_down = push(ts.at[down, 0:64, cs], tr.at[1, 0:64, cs], i + 3, hdev(3))
        first.append((far_up, far_down, plain_up, plain_down))
        ts[h, :, lo:lo + n] = dot(af[h], cf[:, lo:lo + n], 0, 0).astype(BF)
    for r in rings_b:
        r.send(1)
    ring_cr.send(2)
    last = []
    for p, (lo, n) in enumerate(parts):
        cs = pl.ds(lo, n)
        first[p][0].wait_recv()
        tg[0, :, lo:lo + n] = (tf[0, :, lo:lo + n].astype(F32) + ts[up, 0:64, lo:lo + n].astype(F32)).astype(BF)
        last.append(push(tg.at[0, :, cs], tr.at[0, 0:64, cs], its[p] + 4, hdev(1)))
        first[p][1].wait_recv()
        tg[1, :, lo:lo + n] = (tf[1, :, lo:lo + n].astype(F32) + ts[down, 64:128, lo:lo + n].astype(F32)).astype(BF)
        last.append(push(tg.at[1, :, cs], tr.at[1, 64:128, cs], its[p] + 5, hdev(3)))
        for r in rings_b:
            r.send(2 + p)
    ring_cr.send(3)
    for p in range(2):
        first[p][2].wait_recv()
        first[p][3].wait_recv()
    for cp in last:
        cp.wait_recv()
    mom = ts[h].astype(F32) + tr[0].astype(F32) + tr[1].astype(F32)
    l_q.wait()
    q_in = basis_in[0]
    rot = dot(q_in, mom.astype(BF), 0, 0).astype(BF)
    for r in rings_b:
        r.finish()
    m2 = dot(rot, bb[...], 1, 0) / forget_count
    eye = lax.broadcasted_iota(jnp.int32, (128, 128), 0) == lax.broadcasted_iota(jnp.int32, (128, 128), 1)
    l_ein.wait()
    l_eout.wait()
    ein = jnp.sum(jnp.where(eye, ein_v[...], 0.0), axis=1, keepdims=True)
    scaled = (m2 / (ein * eout_v[...].reshape(1, cols) + damping)).astype(BF)
    l_w.wait()

    own, fwd = [], [None, None]
    ig = [sems(6), sems(6)]
    for p, (lo, n) in enumerate(parts):
        cs = pl.ds(lo, n)
        back = dot(scaled, bb[lo:lo + n, :], 1, 1).astype(BF)
        upd = dot(q_in, back, 1, 0)
        nw[h, :, lo:lo + n] = (weight[:, lo:lo + n].astype(F32) + step_size * upd).astype(BF)
        a, b = nw.at[h, 0:64, cs], nw.at[h, 64:128, cs]
        own.append([push(a, a, ig[p], hdev(1)), push(b, b, ig[p] + 1, hdev(3)),
                    push(b, b, ig[p] + 2, hdev(1)), push(a, a, ig[p] + 3, hdev(3))])

    def forward(p):
        cs = pl.ds(parts[p][0], parts[p][1])
        own[p][0].wait_recv()
        a = nw.at[down, 0:64, cs]
        one = push(a, a, ig[p] + 4, hdev(1))
        own[p][1].wait_recv()
        b = nw.at[up, 64:128, cs]
        fwd[p] = (one, push(b, b, ig[p] + 5, hdev(3)))

    igr = sems(16)

    def gradients(q):
        g = dot(cr[...], nw[q], 1, 1)
        for s in range(2):
            for p in range(2):
                ct = 2 * s + p
                gs[q * NC + ct] = jnp.concatenate(
                    [g[(4 * p + i) * rc + 16 * s:(4 * p + i) * rc + 16 * s + 16, :] for i in range(4)], axis=0).astype(BF)
                e = (q * NC + ct - t) % 16
                cp = rcopy(gs.at[q * NC + ct], gr.at[e], igr + e, dev(h, q, ct))

                @pl.when(e != 0)
                def _():
                    cp.start()

    p_r = []

    def retained(p):
        lo, n = parts[p]
        tot = dot(ar[0], nw[0, :, lo:lo + n], 1, 0)
        for q in range(1, NH):
            tot = tot + dot(ar[q], nw[q, :, lo:lo + n], 1, 0)
        for j in range(NY):
            rs[j, :, lo:lo + n] = tot[j * rc:(j + 1) * rc, :].astype(BF)
        i = sems(8)
        cs = pl.ds(lo, n)
        for k in (1, 7, 2, 6, 3, 5, 4):
            p_r.append(push(rs.at[(y + k) % NY, :, cs], rr.at[k, :, cs], i + k, ydev(k)))

    forward(0)
    for cp in g_ar:
        cp.wait_recv()
    ring_cr.finish()
    gradients(h)
    forward(1)
    for cp in (own[0][2], own[0][3]) + fwd[0]:
        cp.wait_recv()
    retained(0)
    for cp in (own[1][2], own[1][3]):
        cp.wait_recv()
    gradients(up)
    gradients(down)
    for cp in fwd[1]:
        cp.wait_recv()
    gradients(far)
    retained(1)

    gsum = gs[t].astype(F32)
    for e in range(1, 16):
        rcopy(gs.at[0], gr.at[e], igr + e, ydev(1)).wait_recv()
        gsum = gsum + gr[e].astype(F32)
    g2[...] = gsum.astype(BF)

    i2 = sems(8)
    s2 = sems(4)

    def own_part(i):
        yo = 4 * core + i
        k = (yo - y) % NY
        return k, pltpu.make_async_remote_copy(
            src_ref=g2.at[i * 16:(i + 1) * 16], dst_ref=g3.at[y], send_sem=ssem.at[s2 + i], recv_sem=rsem.at[i2 + k],
            device_id=(yo * NH + h, t), device_id_type=MESH)

    for i in range(4):
        k, cp = own_part(i)

        @pl.when(k != 0)
        def _():
            cp.start()

        @pl.when(k == 0)
        def _():
            g3[y] = g2[i * 16:(i + 1) * 16, :]

    i3 = sems(8)
    s3 = sems(16)
    mine = (y // 4) == core

    def final(k):
        return pltpu.make_async_remote_copy(
            src_ref=g3, dst_ref=go.at[2 * x + half], send_sem=ssem.at[s3 + k], recv_sem=rsem.at[i3 + 2 * x + half],
            device_id=tdev(k), device_id_type=MESH)

    @pl.when(mine)
    def _():
        for k in range(1, NY):
            rcopy(g2.at[0:16], g3.at[y], i2 + k, ydev(1)).wait_recv()
        for k in (1, 15, 2, 14, 3, 13, 4, 12, 5, 11, 6, 10, 7, 9, 8):
            final(k).start()
        go[2 * x + half] = g3[...]

    for cp in p_r:
        cp.wait_recv()
    tot = rs[y].astype(F32)
    for k in range(1, NY):
        tot = tot + rr[k].astype(F32)
    out_r[...] = tot.astype(BF)

    for cp in pending:
        cp.wait_send()
    for e in range(1, 16):
        rcopy(gs.at[0], gr.at[e], igr + e, ydev(1)).wait_send()
    for i in range(4):
        k, cp = own_part(i)

        @pl.when(k != 0)
        def _():
            cp.wait_send()

    for q in range(NX):
        for s in range(2):
            @pl.when(jnp.logical_not(jnp.logical_and(mine, 2 * x + half == 2 * q + s)))
            def _():
                rcopy(g3, go.at[2 * q + s], i3 + 2 * q + s, ydev(1)).wait_recv()
            for j in range(NY):
                lo = j * dblk + q * 128
                out_g[16 * s:16 * s + 16, lo:lo + 128] = go[2 * q + s, j]

    @pl.when(mine)
    def _():
        for k in range(1, 16):
            final(k).wait_send()
    assert count[0] <= NSEM


def shards(acts, cots, weight, basis_in, basis_out, eigen_in, eigen_out, forget_rows, retain_rows):
    fc, rc = forget_rows.shape[0], retain_rows.shape[0]
    pool, cols = cots.shape
    dim = acts.shape[1]
    dblk = dim // NY
    brows = basis_out.shape[1]
    vm = lambda *s: pltpu.VMEM(s, BF)
    vf = lambda *s: pltpu.VMEM(s, F32)
    kern = functools.partial(body, fc, rc, cols, dblk, brows, float(fc * NY * NH))
    return pl.pallas_call(
        kern,
        out_shape=(jax.ShapeDtypeStruct((rc, cols), BF), jax.ShapeDtypeStruct((rc, dim), BF)),
        in_specs=[pl.BlockSpec(memory_space=pl.ANY)] * 9,
        out_specs=(pl.BlockSpec(memory_space=pltpu.VMEM),) * 2,
        scratch_shapes=[
            vm(pool, NY * 128), vm(pool, cols), vm(128, cols), vm(1, 128, 128), vm(1, brows, cols),
            vf(1, 128), vf(cols), pltpu.VMEM((1, fc), jnp.int32), pltpu.VMEM((1, rc), jnp.int32),
            vm(NH, NY * fc, 128), vm(NH, NY * rc, 128), vm(NY, fc, 128), vm(NY, rc, 128),
            vm(NY * fc, cols), vm(NY * rc, cols),
            vm(NH * 32, cols), vf(NH * brows, cols), vm(cols, cols),
            vm(NH, 128, cols), vm(2, 64, cols), vm(2, 64, cols), vm(2, 128, cols), vm(NH, 128, cols),
            vm(NY, rc, cols), vm(NY, rc, cols),
            vm(16, 64, 128), vm(16, 64, 128), vm(64, 128), vm(NY, 16, 128), vm(2 * NX, NY, 16, 128),
            pltpu.SemaphoreType.DMA((20,)), pltpu.SemaphoreType.DMA((NSEM,)), pltpu.SemaphoreType.DMA((NSEM,)),
        ],
        compiler_params=pltpu.CompilerParams(collective_id=0, has_side_effects=True, vmem_limit_bytes=62 * 2**20),
        name="newton_step",
    )(acts, cots, weight, basis_in, basis_out, eigen_in.reshape(1, -1), eigen_out,
      forget_rows.reshape(1, -1), retain_rows.reshape(1, -1))


def solution(mesh):
    placed = (
        P("fsdp", None),
        P("fsdp", "tp"),
        P("fsdp", "tp"),
        P("fsdp", None, None),
        P("tp", "fsdp", None),
        P("fsdp"),
        P("tp"),
        P("fsdp"),
        P("fsdp"),
    )
    return jax.shard_map(
        shards,
        mesh=mesh,
        in_specs=placed,
        out_specs=(P("fsdp", "tp"), P("fsdp", None)),
        check_vma=False,
    )
```

```python
import functools

import jax
import jax.numpy as jnp
from jax import lax
from jax.experimental import pallas as pl
from jax.experimental.pallas import tpu as pltpu
from jax.sharding import PartitionSpec as P

damping = 0.1
step_size = 0.5
MESH = pl.DeviceIdType.MESH
BF = jnp.bfloat16
F32 = jnp.float32
NY, NH, NX, NC = 8, 4, 4, 4
NSEM = 200


def dot(a, b, ca, cb):
    return lax.dot_general(a, b, (((ca,), (cb,)), ((), ())), preferred_element_type=F32)


def body(fc, rc, cols, dblk, brows, forget_count,
         acts_in, cots_in, weight_in, basis_in_in, basis_out_in, eigen_in_in, eigen_out_in, frow_in, rrow_in,
         out_r, out_g,
         acb, cots, weight, basis_in, bsrc, ein_v, eout_v, frow, rrow,
         af, ar, asf, asr, cf, cr, bz, b112, bb, ts, tf, tg, tr, nw, rs, rr, gs, gr, g2, g3, go,
         lsem, ssem, rsem):
    f = lax.axis_index("fsdp")
    t = lax.axis_index("tp")
    y, h = f // NH, f % NH
    x, c = t // NC, t % NC
    half, core = c // 2, c % 2

    def dev(h_, x_, c_):
        return (y * NH + h_, x_ * NC + c_)

    def ydev(k):
        return (((y + k) % NY) * NH + h, t)

    def hdev(k):
        return dev((h + k) % NH, x, c)

    def tdev(k):
        return (f, (t + k) % 16)

    loads = []

    def load(src, dst):
        cp = pltpu.make_async_copy(src, dst, lsem.at[len(loads)])
        cp.start()
        loads.append(cp)
        return cp

    l_fr = load(frow_in, frow)
    l_rr = load(rrow_in, rrow)
    l_cots = load(cots_in, cots)
    l_acts = [load(acts_in.at[:, pl.ds(pl.multiple_of(j * dblk + x * 128, 128), 128)], acb.at[:, j * 128:(j + 1) * 128])
              for j in range(NY)]
    l_b = load(basis_out_in, bsrc)
    l_w = load(weight_in, weight)
    l_q = load(basis_in_in, basis_in)
    l_ein = load(eigen_in_in, ein_v)
    l_eout = load(eigen_out_in, eout_v)

    bar = pltpu.get_barrier_semaphore()
    peers = [ydev(k) for k in range(1, NY)] + [hdev(k) for k in range(1, NH)] + [tdev(k) for k in range(1, 16)]
    for p in peers:
        pl.semaphore_signal(bar, inc=1, device_id=p, device_id_type=MESH)

    count = [0]

    def sems(n):
        i = count[0]
        count[0] += n
        return i

    def rcopy(src, dst, i, to):
        return pltpu.make_async_remote_copy(
            src_ref=src, dst_ref=dst, send_sem=ssem.at[i], recv_sem=rsem.at[i],
            device_id=to, device_id_type=MESH)

    pending = []

    def push(src, dst, i, to):
        cp = rcopy(src, dst, i, to)
        cp.start()
        pending.append(cp)
        return cp

    def rows_of(slot, n):
        return pl.ds(pl.multiple_of(slot * n, 16), n)

    class Ring:
        def __init__(self, buf, rows, part, first=0, n=None, cs=None):
            self.buf, self.rows, self.part = buf, rows, part
            self.first, self.n = first, rows if n is None else n
            self.cs = pl.ds(0, cols) if cs is None else cs
            self.base = sems(8)
            self.cps = [[], []]

        def send(self, s):
            for d in range(2):
                if s:
                    self.cps[d][s - 1].wait_recv()
                slot = (y - s) % NY if d == 0 else (y + s) % NY
                lo, n = self.first, self.n
                if s == 3:
                    lo, n = (lo, self.part) if d == 0 else (lo + self.part, n - self.part)
                sl = self.buf.at[pl.ds(pl.multiple_of(slot * self.rows + lo, 16), n), self.cs]
                self.cps[d].append(push(sl, sl, self.base + d * 4 + s, ydev(1 if d == 0 else NY - 1)))

        def finish(self):
            for d in range(2):
                self.cps[d][3].wait_recv()

    pool = acb.shape[0]
    l_fr.wait()
    l_rr.wait()
    ohf = (lax.broadcasted_iota(jnp.int32, (pool, fc), 0) == frow[...]).astype(BF)
    ohr = (lax.broadcasted_iota(jnp.int32, (pool, rc), 0) == rrow[...]).astype(BF)
    l_cots.wait()
    cf[rows_of(y, fc), :] = dot(ohf, cots[...], 0, 0).astype(BF)
    for cp in l_acts:
        cp.wait()
    sel = dot(ohf, acb[...], 0, 0).astype(BF)
    for j in range(NY):
        asf[j] = sel[:, j * 128:(j + 1) * 128]
    l_b.wait()
    mine_b = rows_of(h, 32)
    bz[mine_b, :] = jnp.zeros((32, cols), BF)
    bz[pl.ds(pl.multiple_of(h * 32, 16), brows), :] = bsrc[0]
    pl.semaphore_wait(bar, len(peers))

    parts = ((0, 512), (512, cols - 512))
    i = sems(8)
    p_af = [push(asf.at[(y + k) % NY], af.at[x, rows_of(y, fc)], i + k, ydev(k)) for k in (1, 7, 2, 6, 3, 5, 4)]
    rings_cf = [Ring(cf, fc, fc // 2, cs=pl.ds(lo, n)) for lo, n in parts]
    for r in rings_cf:
        r.send(0)
    i = sems(3)
    g_b = [push(bz.at[mine_b], bz.at[mine_b], i + k - 1, hdev(k)) for k in (1, 3, 2)]
    af[x, rows_of(y, fc), :] = asf[y]
    sel = dot(ohr, acb[...], 0, 0).astype(BF)
    for j in range(NY):
        asr[j] = sel[:, j * 128:(j + 1) * 128]
    cr[rows_of(y, rc), :] = dot(ohr, cots[...], 0, 0).astype(BF)
    for cp in p_af:
        cp.wait_recv()
    i = sems(3)
    g_af = [push(af.at[x], af.at[x], i + k - 1, dev(h, (x + k) % NX, c)) for k in (1, 3, 2)]
    for r in rings_cf:
        r.send(1)
    i = sems(8)
    p_ar = [push(asr.at[(y + k) % NY], ar.at[x, rows_of(y, rc)], i + k, ydev(k)) for k in (1, 7, 2, 6, 3, 5, 4)]
    ring_cr = Ring(cr, rc, rc // 2)
    ring_cr.send(0)
    ar[x, rows_of(y, rc), :] = asr[y]
    for cp in g_b:
        cp.wait_recv()
    b112[...] = jnp.concatenate([bz[k * 32:k * 32 + brows, :].astype(F32) for k in range(NH)], axis=0)
    bb[rows_of(y, NH * brows), :] = b112[...].astype(BF)
    rings_b = [Ring(bb, NH * brows, 32, 0, 64), Ring(bb, NH * brows, 32, 64, NH * brows - 64)]
    for r in rings_cf:
        r.send(2)
    ring_cr.send(1)
    for r in rings_cf:
        r.send(3)
    for r in rings_b:
        r.send(0)
    for cp in p_ar:
        cp.wait_recv()
    i = sems(3)
    for cp in g_af:
        cp.wait_recv()
    g_ar = [push(ar.at[x], ar.at[x], i + k - 1, dev(h, (x + k) % NX, c)) for k in (1, 3, 2)]

    up, down, far = (h + 1) % NH, (h + 3) % NH, (h + 2) % NH
    its, first = [], []
    for p, (lo, n) in enumerate(parts):
        cs = pl.ds(lo, n)
        rings_cf[p].finish()
        i = sems(6)
        its.append(i)
        ts[far, :, lo:lo + n] = dot(af[far], cf[:, lo:lo + n], 0, 0).astype(BF)
        far_up = push(ts.at[far, 0:64, cs], tf.at[0, :, cs], i, hdev(1))
        far_down = push(ts.at[far, 64:128, cs], tf.at[1, :, cs], i + 1, hdev(3))
        ts[up, :, lo:lo + n] = dot(af[up], cf[:, lo:lo + n], 0, 0).astype(BF)
        plain_up = push(ts.at[up, 64:128, cs], tr.at[0, 64:128, cs], i + 2, hdev(1))
        ts[down, :, lo:lo + n] = dot(af[down], cf[:, lo:lo + n], 0, 0).astype(BF)
        plain_down = push(ts.at[down, 0:64, cs], tr.at[1, 0:64, cs], i + 3, hdev(3))
        first.append((far_up, far_down, plain_up, plain_down))
        ts[h, :, lo:lo + n] = dot(af[h], cf[:, lo:lo + n], 0, 0).astype(BF)
    ring_cr.send(2)
    for r in rings_b:
        r.send(1)
    last = []
    for p, (lo, n) in enumerate(parts):
        cs = pl.ds(lo, n)
        first[p][0].wait_recv()
        tg[0, :, lo:lo + n] = (tf[0, :, lo:lo + n].astype(F32) + ts[up, 0:64, lo:lo + n].astype(F32)).astype(BF)
        last.append(push(tg.at[0, :, cs], tr.at[0, 0:64, cs], its[p] + 4, hdev(1)))
        first[p][1].wait_recv()
        tg[1, :, lo:lo + n] = (tf[1, :, lo:lo + n].astype(F32) + ts[down, 64:128, lo:lo + n].astype(F32)).astype(BF)
        last.append(push(tg.at[1, :, cs], tr.at[1, 64:128, cs], its[p] + 5, hdev(3)))
        for r in rings_b:
            r.send(2 + p)
    ring_cr.send(3)
    for p in range(2):
        first[p][2].wait_recv()
        first[p][3].wait_recv()
    for cp in last:
        cp.wait_recv()
    mom = ts[h].astype(F32) + tr[0].astype(F32) + tr[1].astype(F32)
    l_q.wait()
    q_in = basis_in[0]
    rot = dot(q_in, mom.astype(BF), 0, 0).astype(BF)
    for r in rings_b:
        r.finish()
    m2 = dot(rot, bb[...], 1, 0) / forget_count
    eye = lax.broadcasted_iota(jnp.int32, (128, 128), 0) == lax.broadcasted_iota(jnp.int32, (128, 128), 1)
    l_ein.wait()
    l_eout.wait()
    ein = jnp.sum(jnp.where(eye, ein_v[...], 0.0), axis=1, keepdims=True)
    scaled = (m2 / (ein * eout_v[...].reshape(1, cols) + damping)).astype(BF)
    l_w.wait()

    own, fwd = [], [None, None]
    ig = [sems(6), sems(6)]
    for p, (lo, n) in enumerate(parts):
        cs = pl.ds(lo, n)
        back = dot(scaled, bb[lo:lo + n, :], 1, 1).astype(BF)
        upd = dot(q_in, back, 1, 0)
        nw[h, :, lo:lo + n] = (weight[:, lo:lo + n].astype(F32) + step_size * upd).astype(BF)
        a, b = nw.at[h, 0:64, cs], nw.at[h, 64:128, cs]
        own.append([push(a, a, ig[p], hdev(1)), push(b, b, ig[p] + 1, hdev(3)),
                    push(b, b, ig[p] + 2, hdev(1)), push(a, a, ig[p] + 3, hdev(3))])

    def forward(p):
        cs = pl.ds(parts[p][0], parts[p][1])
        own[p][0].wait_recv()
        a = nw.at[down, 0:64, cs]
        one = push(a, a, ig[p] + 4, hdev(1))
        own[p][1].wait_recv()
        b = nw.at[up, 64:128, cs]
        fwd[p] = (one, push(b, b, ig[p] + 5, hdev(3)))

    igr = sems(16)

    def gradients(q):
        g = dot(cr[...], nw[q], 1, 1)
        for s in range(2):
            for p in range(2):
                ct = 2 * s + p
                gs[q * NC + ct] = jnp.concatenate(
                    [g[(4 * p + i) * rc + 16 * s:(4 * p + i) * rc + 16 * s + 16, :] for i in range(4)], axis=0).astype(BF)
                e = (q * NC + ct - t) % 16
                cp = rcopy(gs.at[q * NC + ct], gr.at[e], igr + e, dev(h, q, ct))

                @pl.when(e != 0)
                def _():
                    cp.start()

    p_r = []

    def retained(p):
        lo, n = parts[p]
        tot = dot(ar[0], nw[0, :, lo:lo + n], 1, 0)
        for q in range(1, NH):
            tot = tot + dot(ar[q], nw[q, :, lo:lo + n], 1, 0)
        for j in range(NY):
            rs[j, :, lo:lo + n] = tot[j * rc:(j + 1) * rc, :].astype(BF)
        i = sems(8)
        cs = pl.ds(lo, n)
        for k in (1, 7, 2, 6, 3, 5, 4):
            p_r.append(push(rs.at[(y + k) % NY, :, cs], rr.at[k, :, cs], i + k, ydev(k)))

    forward(0)
    for cp in g_ar:
        cp.wait_recv()
    ring_cr.finish()
    gradients(h)
    forward(1)
    for cp in (own[0][2], own[0][3]) + fwd[0]:
        cp.wait_recv()
    retained(0)
    for cp in (own[1][2], own[1][3]):
        cp.wait_recv()
    gradients(up)
    gradients(down)
    for cp in fwd[1]:
        cp.wait_recv()
    gradients(far)

    gsum = gs[t].astype(F32)
    for e in range(1, 16):
        rcopy(gs.at[0], gr.at[e], igr + e, ydev(1)).wait_recv()
        gsum = gsum + gr[e].astype(F32)
    g2[...] = gsum.astype(BF)

    i2 = sems(8)
    s2 = sems(4)

    def own_part(i):
        yo = 4 * core + i
        k = (yo - y) % NY
        return k, pltpu.make_async_remote_copy(
            src_ref=g2.at[i * 16:(i + 1) * 16], dst_ref=g3.at[y], send_sem=ssem.at[s2 + i], recv_sem=rsem.at[i2 + k],
            device_id=(yo * NH + h, t), device_id_type=MESH)

    for i in range(4):
        k, cp = own_part(i)

        @pl.when(k != 0)
        def _():
            cp.start()

        @pl.when(k == 0)
        def _():
            g3[y] = g2[i * 16:(i + 1) * 16, :]

    retained(1)

    i3 = sems(8)
    s3 = sems(16)
    mine = (y // 4) == core

    def final(k):
        return pltpu.make_async_remote_copy(
            src_ref=g3, dst_ref=go.at[2 * x + half], send_sem=ssem.at[s3 + k], recv_sem=rsem.at[i3 + 2 * x + half],
            device_id=tdev(k), device_id_type=MESH)

    @pl.when(mine)
    def _():
        for k in range(1, NY):
            rcopy(g2.at[0:16], g3.at[y], i2 + k, ydev(1)).wait_recv()
        for k in (1, 15, 2, 14, 3, 13, 4, 12, 5, 11, 6, 10, 7, 9, 8):
            final(k).start()
        go[2 * x + half] = g3[...]

    for cp in p_r:
        cp.wait_recv()
    tot = rs[y].astype(F32)
    for k in range(1, NY):
        tot = tot + rr[k].astype(F32)
    out_r[...] = tot.astype(BF)

    for cp in pending:
        cp.wait_send()
    for e in range(1, 16):
        rcopy(gs.at[0], gr.at[e], igr + e, ydev(1)).wait_send()
    for i in range(4):
        k, cp = own_part(i)

        @pl.when(k != 0)
        def _():
            cp.wait_send()

    for q in range(NX):
        for s in range(2):
            @pl.when(jnp.logical_not(jnp.logical_and(mine, 2 * x + half == 2 * q + s)))
            def _():
                rcopy(g3, go.at[2 * q + s], i3 + 2 * q + s, ydev(1)).wait_recv()
            for j in range(NY):
                lo = j * dblk + q * 128
                out_g[16 * s:16 * s + 16, lo:lo + 128] = go[2 * q + s, j]

    @pl.when(mine)
    def _():
        for k in range(1, 16):
            final(k).wait_send()
    assert count[0] <= NSEM


def shards(acts, cots, weight, basis_in, basis_out, eigen_in, eigen_out, forget_rows, retain_rows):
    fc, rc = forget_rows.shape[0], retain_rows.shape[0]
    pool, cols = cots.shape
    dim = acts.shape[1]
    dblk = dim // NY
    brows = basis_out.shape[1]
    vm = lambda *s: pltpu.VMEM(s, BF)
    vf = lambda *s: pltpu.VMEM(s, F32)
    kern = functools.partial(body, fc, rc, cols, dblk, brows, float(fc * NY * NH))
    return pl.pallas_call(
        kern,
        out_shape=(jax.ShapeDtypeStruct((rc, cols), BF), jax.ShapeDtypeStruct((rc, dim), BF)),
        in_specs=[pl.BlockSpec(memory_space=pl.ANY)] * 9,
        out_specs=(pl.BlockSpec(memory_space=pltpu.VMEM),) * 2,
        scratch_shapes=[
            vm(pool, NY * 128), vm(pool, cols), vm(128, cols), vm(1, 128, 128), vm(1, brows, cols),
            vf(1, 128), vf(cols), pltpu.VMEM((1, fc), jnp.int32), pltpu.VMEM((1, rc), jnp.int32),
            vm(NH, NY * fc, 128), vm(NH, NY * rc, 128), vm(NY, fc, 128), vm(NY, rc, 128),
            vm(NY * fc, cols), vm(NY * rc, cols),
            vm(NH * 32, cols), vf(NH * brows, cols), vm(cols, cols),
            vm(NH, 128, cols), vm(2, 64, cols), vm(2, 64, cols), vm(2, 128, cols), vm(NH, 128, cols),
            vm(NY, rc, cols), vm(NY, rc, cols),
            vm(16, 64, 128), vm(16, 64, 128), vm(64, 128), vm(NY, 16, 128), vm(2 * NX, NY, 16, 128),
            pltpu.SemaphoreType.DMA((20,)), pltpu.SemaphoreType.DMA((NSEM,)), pltpu.SemaphoreType.DMA((NSEM,)),
        ],
        compiler_params=pltpu.CompilerParams(collective_id=0, has_side_effects=True, vmem_limit_bytes=62 * 2**20),
        name="newton_step",
    )(acts, cots, weight, basis_in, basis_out, eigen_in.reshape(1, -1), eigen_out,
      forget_rows.reshape(1, -1), retain_rows.reshape(1, -1))


def solution(mesh):
    placed = (
        P("fsdp", None),
        P("fsdp", "tp"),
        P("fsdp", "tp"),
        P("fsdp", None, None),
        P("tp", "fsdp", None),
        P("fsdp"),
        P("tp"),
        P("fsdp"),
        P("fsdp"),
    )
    return jax.shard_map(
        shards,
        mesh=mesh,
        in_specs=placed,
        out_specs=(P("fsdp", "tp"), P("fsdp", None)),
        check_vma=False,
    )
```
